32 devices in a mesh: batch: 4 (over y, x), seq: 8 (over z, core).
Axes of the slice: x: 2, y: 2, z: 4, core: 2. Of those that a mesh axis runs over, the one named last changes fastest.
Arguments:
- hidden_in: bfloat16 [8, 1024, 2048], P('batch', 'seq'), may hold values from -6 to 6
- lengths: int32 [8], replicated, may hold values from 256 to 1024, as said below
- q_weight: bfloat16 [2048, 256], P(('batch', 'seq')), may hold values from -0.125 to 0.125
- k_weight: bfloat16 [2048, 256], P(('batch', 'seq')), may hold values from -0.125 to 0.125
- v_weight: bfloat16 [2048, 2048], P(('batch', 'seq')), may hold values from -0.125 to 0.125
- out_weight: bfloat16 [2048, 2048], P(None, ('batch', 'seq')), may hold values from -2 to 2
- conv_weight: bfloat16 [2048, 3], P(('batch', 'seq')), may hold values from -3 to 3
- norm_attn: bfloat16 [2048], P(('batch', 'seq')), may hold values from 0.099609375 to 1.8984375
- gate_weight: bfloat16 [2048, 5504], P(('batch', 'seq')), may hold values from -0.125 to 0.125
- up_weight: bfloat16 [2048, 5504], P(('batch', 'seq')), may hold values from -0.125 to 0.125
- down_weight: bfloat16 [5504, 2048], P(None, ('batch', 'seq')), may hold values from -0.078125 to 0.078125
- norm_mlp: bfloat16 [2048], P(('batch', 'seq')), may hold values from 0.099609375 to 1.8984375
- cotangent: bfloat16 [8, 1024, 2048], P('batch', 'seq'), may hold values from -6 to 6
Outputs:
- hidden_out: bfloat16 [8, 1024, 2048], P('batch', 'seq')
- hidden_grad: float32 [8, 1024, 2048], P('batch', 'seq')
- grad_q: float32 [2048, 256], P(('batch', 'seq'))
- grad_k: float32 [2048, 256], P(('batch', 'seq'))
- grad_v: float32 [2048, 2048], P(('batch', 'seq'))
- grad_out: float32 [2048, 2048], P(None, ('batch', 'seq'))
- grad_conv: float32 [2048, 3], P(('batch', 'seq'))
- grad_norm_attn: float32 [2048], P(('batch', 'seq'))
- grad_gate: float32 [2048, 5504], P(('batch', 'seq'))
- grad_up: float32 [2048, 5504], P(('batch', 'seq'))
- grad_down: float32 [5504, 2048], P(None, ('batch', 'seq'))
- grad_norm_mlp: float32 [2048], P(('batch', 'seq'))
- den_mean: float32 [], replicated
The draws below stay inside these ranges and needn't reach their ends.
Inputs may be any that keep to these rules, and one draw needn't show every extreme that they name: `lengths`: valid tokens of each sequence counted from its start; later positions are padding. Among the sequences of each index of batch one has 1024 valid tokens.
All inputs are finite; a program needn't handle non-finite values.
Results may differ from the reference program's by a relative error of at most 0.017.
Values may be sent and summed in bfloat16 or wider, within the bound.
No kernel may reach another device: no remote copies, remote signals or barrier semaphores. Data moves between devices by JAX's collectives and lax.ppermute only.
A program may use at most 512 MiB of HBM per device.

```python
import math
import jax
import jax.numpy as jnp
from jax import lax

D = 2048
HEADS = 16
FEAT = 16
FF = 5504
KERNEL = 3
ROWS_DEV = 2
PHI = 273
HV = 128
HK = 256
SEQ_LEN = 1024
SEQS = 8


def draw_lengths(key, part):
    key = jax.random.fold_in(key, 11)
    key_rand, key_perm = jax.random.split(key)
    groups = SEQS // ROWS_DEV
    group_ids = jnp.arange(groups, dtype=jnp.int32)[:, None]
    lowest = SEQ_LEN // 4 + SEQ_LEN // 2 * group_ids // max(groups - 1, 1)
    drawn = lowest + jax.random.randint(key_rand, (groups, ROWS_DEV), 0, SEQ_LEN // 4 + 1, dtype=jnp.int32)
    drawn = jnp.minimum(drawn, SEQ_LEN)
    column = jnp.arange(ROWS_DEV, dtype=jnp.int32)[None, :]
    base_len = jnp.where(column == 0, SEQ_LEN, drawn)
    shuffled = jax.vmap(jax.random.permutation)(jax.random.split(key_perm, groups), base_len)
    return shuffled.reshape(SEQS).astype(jnp.int32)


def with_spikes(result, rng, source, target, blocks, factor):
    def block_of(position):
        return (jnp.arange(result.shape[position]) // (result.shape[position] // blocks)).reshape((-1,) + (1,) * (result.ndim - 1 - position))

    near = jax.random.permutation(rng, blocks)[block_of(target)]
    far = (block_of(target) + blocks // 2) % blocks
    return jnp.where((block_of(source) == near) | (block_of(source) == far), factor * result, result)


def block_levels(rng, extent, cuts, low, top_value):
    def one(axis_at, shards_of):
        steps = jax.random.uniform(jax.random.fold_in(jax.random.fold_in(rng, 6), axis_at), (shards_of,), jnp.float32, low / len(cuts), top_value / len(cuts))
        return jnp.repeat(jnp.exp(steps), extent[axis_at] // shards_of).reshape((-1,) + (1,) * (len(extent) - axis_at - 1))

    loudness = one(*cuts[0])
    for cut in cuts[1:]:
        loudness = loudness * one(*cut)
    return loudness


def scatter_about(rng, dims, scale, reach, cuts=(), held_as=jnp.bfloat16):
    result = scale * jax.random.normal(rng, dims, jnp.float32)
    if cuts:
        result = result * block_levels(rng, dims, cuts, -0.22, 0.18)
    return jnp.clip(result, -reach, reach).astype(held_as)


def heavy_noise(key, shape, spread, bound, shards, heavy, kind=jnp.bfloat16):
    result = spread * jax.random.normal(key, shape, jnp.float32)
    if shards:
        result = result * block_levels(key, shape, shards, -0.22, 0.18)
    return jnp.clip(with_spikes(result, jax.random.fold_in(key, 3), *heavy), -bound, bound).astype(kind)


def setup_inputs(seed: int = 0) -> dict:
    seeds = jax.random.split(jax.random.key(seed), 14)
    hidden_in = scatter_about(seeds[0], (SEQS, SEQ_LEN, D), 1.0, 6.0, ((0, 4), (1, 8)))
    lengths = draw_lengths(jax.random.fold_in(seeds[13], 71), 0)
    q_weight = scatter_about(seeds[2], (D, HK), D ** -0.5, 0.125, ((0, 32),))
    k_weight = scatter_about(seeds[3], (D, HK), D ** -0.5, 0.125, ((0, 32),))
    v_weight = scatter_about(seeds[4], (D, D), D ** -0.5, 0.125, ((0, 32),))
    out_weight = scatter_about(seeds[5], (D, D), 8 ** -0.5, 2.0, ((1, 32),))
    conv_weight = scatter_about(seeds[6], (D, KERNEL), 0.6, 3.0, ((0, 32),))
    norm_attn = jnp.clip(1.0 + 0.18 * jax.random.normal(seeds[7], (D,), jnp.float32), 0.099609375, 1.8984375).astype(jnp.bfloat16)
    gate_weight = scatter_about(seeds[8], (D, FF), D ** -0.5, 0.125, ((0, 32),))
    up_weight = scatter_about(seeds[9], (D, FF), D ** -0.5, 0.125, ((0, 32),))
    down_weight = scatter_about(seeds[10], (FF, D), FF ** -0.5, 0.078125, ((1, 32),))
    norm_mlp = jnp.clip(1.0 + 0.18 * jax.random.normal(seeds[11], (D,), jnp.float32), 0.099609375, 1.8984375).astype(jnp.bfloat16)
    cotangent = heavy_noise(seeds[12], (SEQS, SEQ_LEN, D), 1.0, 6.0, ((0, 4), (1, 8)), (1, 2, 8, 2.0))
    return dict(hidden_in=hidden_in, lengths=lengths, q_weight=q_weight, k_weight=k_weight, v_weight=v_weight, out_weight=out_weight, conv_weight=conv_weight, norm_attn=norm_attn, gate_weight=gate_weight, up_weight=up_weight, down_weight=down_weight, norm_mlp=norm_mlp, cotangent=cotangent)


epsilon = 1e-06
highest = lax.Precision.HIGHEST

@jax.custom_vjp
def low(v):
    return lax.optimization_barrier(v.astype(jnp.bfloat16)).astype(jnp.float32)

@jax.custom_vjp
def low_back(v):
    return v

def low_keep(v):
    return (low(v), None)

def low_pass(kept, grad):
    return (grad,)

def back_keep(v):
    return (v, None)

def back_low(kept, grad):
    return (low(grad),)
low.defvjp(low_keep, low_pass)
low_back.defvjp(back_keep, back_low)

def matmul(left, right):
    return jnp.dot(left, right, precision=highest, preferred_element_type=jnp.float32)

def rms_norm(v, gain):
    return v * lax.rsqrt(lax.optimization_barrier(jnp.mean(v * v, axis=-1, keepdims=True)) + epsilon) * gain

def features(u):
    feat_width = u.shape[-1]
    quad_terms = (u[..., :, None] * u[..., None, :]).reshape(u.shape[:-1] + (feat_width * feat_width,))
    ones_col = jnp.ones(u.shape[:-1] + (1,), u.dtype)
    return jnp.concatenate([ones_col, u * feat_width ** (-0.25), quad_terms / math.sqrt(2.0 * feat_width)], axis=-1)

def attend(feat_q, feat_k, v_low):
    block_len = min(512, SEQ_LEN)
    block_count = SEQ_LEN // block_len
    causal = jnp.tril(jnp.ones((block_len, block_len), feat_q.dtype))

    def block_step(carried, blocks):
        prev_state, prev_total = carried
        blk_q, blk_k, blk_v = blocks
        scores = jnp.einsum('thp,shp->hts', blk_q, blk_k, precision=highest) * causal
        numerator = jnp.einsum('hts,shv->thv', scores, blk_v, precision=highest) + jnp.einsum('thp,hpv->thv', blk_q, prev_state, precision=highest)
        denominator = lax.optimization_barrier(jnp.sum(scores, axis=-1)).T + jnp.einsum('thp,hp->th', blk_q, prev_total, precision=highest)
        prev_state = prev_state + jnp.einsum('shp,shv->hpv', blk_k, blk_v, precision=highest)
        prev_total = prev_total + lax.optimization_barrier(jnp.sum(blk_k, axis=0))
        return ((prev_state, prev_total), (numerator, denominator))

    def to_blocks(arr):
        return arr.reshape((block_count, block_len) + arr.shape[1:])
    initial = (jnp.zeros((HEADS, PHI, HV), feat_q.dtype), jnp.zeros((HEADS, PHI), feat_q.dtype))
    _, (numerator, denominator) = lax.scan(jax.checkpoint(block_step), initial, (to_blocks(feat_q), to_blocks(feat_k), to_blocks(v_low)))
    return (numerator.reshape(SEQ_LEN, HEADS, HV), denominator.reshape(SEQ_LEN, HEADS))

def row_block(weights, x_row, length):
    w_query, w_key, w_value, w_out, w_conv, gain_attn, w_gate, w_up, w_down, gain_mlp = weights
    normed_attn = rms_norm(x_row, gain_attn)
    padded = jnp.concatenate([jnp.zeros((KERNEL - 1, D), normed_attn.dtype), normed_attn], axis=0)
    mixed_in = jnp.zeros_like(normed_attn)
    for j in range(KERNEL):
        mixed_in = mixed_in + w_conv[:, j] * padded[KERNEL - 1 - j:KERNEL - 1 - j + SEQ_LEN]
    c_low = low(mixed_in)
    queries = low_back(matmul(c_low, w_query))
    keys_raw = low_back(matmul(c_low, w_key))
    values = low_back(matmul(c_low, w_value))
    pad_mask = (jnp.arange(SEQ_LEN, dtype=jnp.int32) < length).astype(x_row.dtype)
    feat_q = low(features(queries.reshape(SEQ_LEN, HEADS, FEAT)))
    feat_k = low(features(keys_raw.reshape(SEQ_LEN, HEADS, FEAT))) * pad_mask[:, None, None]
    v_low = low(values).reshape(SEQ_LEN, HEADS, HV)
    numerator, denominator = attend(feat_q, feat_k, v_low)
    attn_val = numerator / denominator[..., None]
    y_low = low(attn_val.reshape(SEQ_LEN, D))
    resid_mid = x_row + low_back(matmul(y_low, w_out))
    n2_low = low(rms_norm(resid_mid, gain_mlp))
    gate_act = low_back(matmul(n2_low, w_gate))
    up_act = low_back(matmul(n2_low, w_up))
    hidden_act = low(jax.nn.silu(gate_act) * up_act)
    block_out = resid_mid + low_back(matmul(hidden_act, w_down))
    return (block_out, jnp.sum(denominator * pad_mask[:, None]))

def reference(hidden_in, lengths, q_weight, k_weight, v_weight, out_weight, conv_weight, norm_attn, gate_weight, up_weight, down_weight, norm_mlp, cotangent):
    weights_f32 = tuple((w.astype(jnp.float32) for w in (q_weight, k_weight, v_weight, out_weight, conv_weight, norm_attn, gate_weight, up_weight, down_weight, norm_mlp)))
    inputs = hidden_in.astype(jnp.float32)

    def forward(weights, rows_in):

        def one_row(row_pair):
            return jax.checkpoint(row_block)(weights, row_pair[0], row_pair[1])
        block_outs, den_sums = lax.map(one_row, (rows_in, lengths))
        return (block_outs, den_sums)
    block_outs, pullback, den_sums = jax.vjp(forward, weights_f32, inputs, has_aux=True)
    grads, grad_in = pullback(cotangent.astype(jnp.float32))
    den_mean = jnp.sum(den_sums) / (HEADS * SEQ_LEN * jnp.sum(lengths).astype(jnp.float32))
    return (block_outs.astype(jnp.bfloat16), grad_in, grads[0], grads[1], grads[2], grads[3], grads[4], grads[5], grads[6], grads[7], grads[8], grads[9], den_mean)
```

```python
import math

import jax
import jax.numpy as jnp
import ml_dtypes
from jax import lax
from jax.experimental import pallas as pl
from jax.experimental.pallas import tpu as pltpu
from jax.sharding import PartitionSpec as P

HEADS = 16
FEAT = 16
KERNEL = 3
LANES = 128
HALF = 64

epsilon = 1e-06
bf16 = jnp.bfloat16
f32 = jnp.float32
alpha = (2.0 * FEAT) ** -0.25
shift = math.sqrt(FEAT) / math.sqrt(2.0 * FEAT)


def rms_norm(v, gain):
    return v * lax.rsqrt(jnp.mean(v * v, axis=-1, keepdims=True) + epsilon) * gain


def contract(left, right, dims, kind=f32):
    return lax.dot_general(left, right, ((dims[:1], dims[1:]), ((), ())), preferred_element_type=kind)


def nn(left, right):
    return contract(left, right, (1, 0))


def nt(left, right):
    return contract(left, right, (1, 1))


def tn(left, right):
    return contract(left, right, (0, 0))


def pick(value, at, axis=0):
    return lax.dynamic_index_in_dim(value, at, axis, False)


class Links:
    def __init__(self):
        self.nb, self.ns = (lax.axis_size("batch"), lax.axis_size("seq"))
        self.nz = self.ns // 2
        self.b = lax.axis_index("batch")
        seq = lax.axis_index("seq")
        self.z, self.c = (seq // 2, seq % 2)
        self.seq = seq

    def core(self, value):
        return lax.ppermute(value, "seq", [(s, s ^ 1) for s in range(self.ns)])

    def ring(self, value):
        return lax.ppermute(value, "seq", [(s, (s + 2) % self.ns) for s in range(self.ns)])

    def across(self, value, d):
        return lax.ppermute(value, "batch", [(b, b ^ d) for b in range(self.nb)])

    def to_seq(self, value, dz, dc):
        return lax.ppermute(
            value,
            "seq",
            [(s, 2 * ((s // 2 + dz) % self.nz) + ((s % 2) ^ dc)) for s in range(self.ns)],
        )

    def behind(self, k):
        return lax.rem(self.z + (self.nz - k), self.nz)

    def gather_plane(self, x):
        h = x.shape[0] // 2
        one, two = (self.across(x, 1), self.across(x, 2))
        three = (self.across(one[:h], 2), self.across(two[h:], 1))
        mine = (x, one, two) + three
        return jnp.concatenate(mine + tuple(self.core(v) for v in mine), axis=0)

    def scatter_plane(self, part):
        s = part[0].astype(f32) + self.core(part[1]).astype(f32)
        h = s.shape[1] // 2
        far = s[3].astype(bf16)
        a, b = (self.across(far[:h], 1), self.across(far[h:], 2))
        to_two = jnp.concatenate([s[2, :h] + a.astype(f32), s[2, h:]], axis=0).astype(bf16)
        to_one = jnp.concatenate([s[1, :h], s[1, h:] + b.astype(f32)], axis=0).astype(bf16)
        return s[0] + self.across(to_one, 1).astype(f32) + self.across(to_two, 2).astype(f32)

    def gather_all(self, x):
        chain = [x]
        for _ in range(self.nz - 1):
            chain.append(self.ring(chain[-1]))
        column = jnp.stack(chain)
        h = self.nz // 2
        one, two = (self.across(column, 1), self.across(column, 2))
        mine = (
            (column, 0, 0),
            (one, 1, 0),
            (two, 2, 0),
            (self.across(one[:h], 2), 3, 0),
            (self.across(two[h:], 1), 3, h),
        )
        items, places = ([], [])
        for dc in range(2):
            for value, d, first in mine:
                got = self.core(value) if dc else value
                for k in range(value.shape[0]):
                    items.append((got, k))
                    places.append((self.behind(first + k) * self.nb + (self.b ^ d)) * 2 + (self.c ^ dc))
        return items, places

    def scatter_all(self, part):
        kind = part.dtype
        got = self.core(pick(part, self.c ^ 1, 2))
        pair = (pick(part, self.c, 2).astype(f32) + got.astype(f32)).astype(kind)
        h = self.nz // 2
        s = [pick(pair, self.b ^ d, 1) for d in range(4)]
        a, b = (self.across(s[3][:h], 1), self.across(s[3][h:], 2))
        to_two = jnp.concatenate([(s[2][:h].astype(f32) + a.astype(f32)).astype(kind), s[2][h:]], axis=0)
        to_one = jnp.concatenate([s[1][:h], (s[1][h:].astype(f32) + b.astype(f32)).astype(kind)], axis=0)
        line = (
            s[0].astype(f32) + self.across(to_one, 1).astype(f32) + self.across(to_two, 2).astype(f32)
        ).astype(kind)
        return self.scatter_ring([pick(line, self.behind(j)) for j in range(self.nz)])

    def scatter_ring(self, parts):
        total = parts[1 % self.nz].astype(f32)
        for j in range(1, self.nz):
            total = self.ring(total.astype(parts[0].dtype)).astype(f32) + parts[(j + 1) % self.nz].astype(f32)
        return total

    def exchange_seq(self, value):
        got, sources = ([], [])
        for dz in range(self.nz):
            for dc in range(2):
                to = 2 * lax.rem(self.z + dz, self.nz) + (self.c ^ dc)
                piece = pick(value, to)
                got.append(self.to_seq(piece, dz, dc) if dz or dc else piece)
                sources.append(2 * self.behind(dz) + (self.c ^ dc))
        return got, sources

    def sum_all(self, value):
        value = value + self.core(value)
        value = value + self.across(value, 1)
        value = value + self.across(value, 2)
        moving = value
        for _ in range(self.nz - 1):
            moving = self.ring(moving)
            value = value + moving
        return value


def assemble(items, places, shape, view):
    arrays, plan = ([], [])
    for value, at in items:
        known = [i for i, a in enumerate(arrays) if a is value]
        if not known:
            arrays.append(value)
            known = [len(arrays) - 1]
        plan.append((known[0], at))
    count = len(arrays)

    def kernel(place, *refs):
        out, sems = (refs[count], refs[count + 1])
        copies = []
        for t, (i, at) in enumerate(plan):
            source = refs[i] if at is None else refs[i].at[at]
            copies.append(pltpu.make_async_copy(source, view(out, place[t]), sems.at[t]))
            copies[-1].start()
        for copy in copies:
            copy.wait()

    size = math.prod(shape)
    return pl.pallas_call(
        kernel,
        out_shape=jax.ShapeDtypeStruct(shape, arrays[0].dtype),
        in_specs=[pl.BlockSpec(memory_space=pltpu.SMEM)] + [pl.BlockSpec(memory_space=pl.ANY)] * count,
        out_specs=pl.BlockSpec(memory_space=pltpu.VMEM),
        scratch_shapes=[pltpu.SemaphoreType.DMA((len(plan),))],
        compiler_params=pltpu.CompilerParams(vmem_limit_bytes=40 * 1024 * 1024),
        cost_estimate=pl.CostEstimate(flops=0, bytes_accessed=4 * size, transcendentals=0),
    )(jnp.stack(places).astype(jnp.int32), *arrays)


def join_rows(items, places, rows, width):
    return assemble(
        items,
        places,
        (len(items) * rows, width),
        lambda out, at: out.at[pl.ds(pl.multiple_of(at * rows, rows), rows)],
    )


def join_lead(parts, places):
    return assemble(
        [(p, None) for p in parts],
        places,
        (len(parts),) + parts[0].shape,
        lambda out, at: out.at[at],
    )


def join_lanes(parts, places):
    width = parts[0].shape[-1]
    if width % LANES:
        whole = jnp.moveaxis(join_lead(parts, places), 0, -2)
        return whole.reshape(whole.shape[:-2] + (len(parts) * width,))
    return assemble(
        [(p, None) for p in parts],
        places,
        parts[0].shape[:-1] + (len(parts) * width,),
        lambda out, at: out.at[:, :, pl.ds(pl.multiple_of(at * width, width), width)],
    )


def sweep(lower, upper, body):
    if isinstance(lower, int) and isinstance(upper, int) and upper - lower <= 4:
        for i in range(lower, upper):
            body(i)
    else:
        lax.fori_loop(lower, upper, lambda i, none: (body(i), none)[1], None)


def rows_at(i, block):
    return pl.ds(i * block if isinstance(i, int) else pl.multiple_of(i * block, block), block)


def lane_of(shape):
    return lax.broadcasted_iota(jnp.int32, shape, 1)


def fetch(places, pieces, target, sems, first, rows):
    copies = []
    for t, piece in enumerate(pieces):
        copies.append(
            pltpu.make_async_copy(
                piece,
                target.at[pl.ds(pl.multiple_of(places[t] * rows, rows), rows)],
                sems.at[first + t],
            )
        )
        copies[-1].start()
    return copies


def prepare(i, block, units, length, qkv, qa, ka, va):
    rows = rows_at(i, block)
    raw = qkv[rows, :LANES].astype(f32)
    lane = lane_of((block, LANES))
    valid = (i * block + lax.broadcasted_iota(jnp.int32, (block, LANES), 0)) < length
    high = float(ml_dtypes.bfloat16(shift))
    keys = jnp.where(
        lane < HALF,
        pltpu.roll(raw, HALF, 1),
        jnp.where(lane == HALF, high, jnp.where(lane == HALF + 1, shift - high, 0.0)),
    )
    ka[rows, :] = jnp.where(valid, keys, 0.0).astype(bf16)
    extra = jnp.where((lane == HALF) | (lane == HALF + 1), 1.0, 0.0)
    ones = jnp.where(valid & (lane < 2), 1.0, 0.0).astype(bf16)
    for u in range(units):
        own = (lane >= u * FEAT) & (lane < (u + 1) * FEAT)
        qa[u, rows, :] = jnp.where(own, raw, extra).astype(bf16)
        v = qkv[rows, pl.ds(LANES * (u + 1), LANES)]
        va[u, rows, :LANES] = jnp.where(valid, v.astype(f32), 0.0).astype(bf16)
        va[u, rows, LANES:] = ones


def lower_triangle(block):
    shape = (block, block)
    return lax.broadcasted_iota(jnp.int32, shape, 0) >= lax.broadcasted_iota(jnp.int32, shape, 1)


def upper_triangle(block):
    shape = (block, block)
    return lax.broadcasted_iota(jnp.int32, shape, 0) <= lax.broadcasted_iota(jnp.int32, shape, 1)


def attend(pieces, sources, length, units, block):
    count = len(pieces)
    rows_each = pieces[0].shape[0]
    total = count * rows_each
    blocks = total // block

    def kernel(places, length_ref, *refs):
        y, attn, den = refs[count : count + 3]
        qkv, qa, ka, va, sems = refs[count + 3 :]
        for copy in fetch(places, refs[:count], qkv, sems, 0, rows_each):
            copy.wait()
        valid_len = length_ref[0]
        sweep(0, blocks, lambda i: prepare(i, block, units, valid_len, qkv, qa, ka, va))

        def one(i):
            rows = rows_at(i, block)
            lane = lane_of((block, LANES))
            den_all = jnp.zeros((block, LANES), f32)
            for u in range(units):

                def term(j, masked=False):
                    s = nt(qa[u, rows, :], ka[rows_at(j, block), :])
                    p = s * s + 0.5
                    if masked:
                        p = jnp.where(lower_triangle(block), p, 0.0)
                    return nn(p.astype(bf16), va[u, rows_at(j, block), :])

                total_u = term(i, True)
                if isinstance(i, int):
                    for j in range(i):
                        total_u = total_u + term(j)
                else:
                    total_u = lax.fori_loop(0, i, lambda j, t: t + term(j), total_u)
                den_u = total_u[:, LANES : LANES + 1]
                out = total_u[:, :LANES] / den_u
                cols = pl.ds(LANES * u, LANES)
                attn[rows, cols] = out
                y[rows, cols] = out.astype(bf16)
                den_all = jnp.where(lane == u, den_u, den_all)
            den[rows, :] = den_all

        sweep(0, blocks, one)

    return pl.pallas_call(
        kernel,
        out_shape=(
            jax.ShapeDtypeStruct((total, LANES * units), bf16),
            jax.ShapeDtypeStruct((total, LANES * units), f32),
            jax.ShapeDtypeStruct((total, LANES), f32),
        ),
        in_specs=[pl.BlockSpec(memory_space=pltpu.SMEM)] * 2 + [pl.BlockSpec(memory_space=pl.ANY)] * count,
        out_specs=[pl.BlockSpec(memory_space=pltpu.VMEM)] * 3,
        scratch_shapes=[
            pltpu.VMEM((total, LANES * (units + 1)), bf16),
            pltpu.VMEM((units, total, LANES), bf16),
            pltpu.VMEM((total, LANES), bf16),
            pltpu.VMEM((units, total, 2 * LANES), bf16),
            pltpu.SemaphoreType.DMA((count,)),
        ],
        compiler_params=pltpu.CompilerParams(vmem_limit_bytes=48 * 1024 * 1024),
        cost_estimate=pl.CostEstimate(
            flops=units * total * total * 400, bytes_accessed=total * 4096, transcendentals=0
        ),
    )(jnp.stack(sources).astype(jnp.int32), length, *pieces)


def attend_back(pieces, sources, length, d_pieces, attn, den, units, block):
    count = len(pieces)
    rows_each = pieces[0].shape[0]
    total = count * rows_each
    blocks = total // block

    def kernel(places, length_ref, *refs):
        attn_ref, den_ref = refs[2 * count : 2 * count + 2]
        out = refs[2 * count + 2]
        qkv, qa, ka, va, dy, dna, dq, dk, dv, sems = refs[2 * count + 3 :]
        copies = fetch(places, refs[:count], qkv, sems, 0, rows_each)
        copies += fetch(places, refs[count : 2 * count], dy, sems, count, rows_each)
        for copy in copies:
            copy.wait()
        valid_len = length_ref[0]

        def ready(i):
            prepare(i, block, units, valid_len, qkv, qa, ka, va)
            rows = rows_at(i, block)
            lane = lane_of((block, LANES))
            for u in range(units):
                cols = pl.ds(LANES * u, LANES)
                inverse = 1.0 / den_ref[rows, u : u + 1]
                grad = dy[rows, cols].astype(f32)
                scaled = -jnp.sum(grad * attn_ref[rows, cols], axis=1, keepdims=True) * inverse
                high = scaled.astype(bf16).astype(f32)
                dna[u, rows, :LANES] = (grad * inverse).astype(bf16)
                dna[u, rows, LANES:] = jnp.where(
                    lane == 0, high, jnp.where(lane == 1, scaled - high, 0.0)
                ).astype(bf16)
            dq[rows, :] = jnp.zeros((block, LANES), f32)
            dk[rows, :] = jnp.zeros((block, LANES), f32)
            dv[rows, :] = jnp.zeros((block, LANES * units), f32)

        sweep(0, blocks, ready)

        def pair(i, j, masked):
            t_rows, s_rows = (rows_at(i, block), rows_at(j, block))
            lane = lane_of((block, LANES))
            for u in range(units):
                q, k, v, g = (qa[u, t_rows, :], ka[s_rows, :], va[u, s_rows, :], dna[u, t_rows, :])
                ds = nt(g, v) * nt(q, k)
                if masked:
                    ds = jnp.where(lower_triangle(block), ds, 0.0)
                own = (lane >= u * FEAT) & (lane < (u + 1) * FEAT)
                dq[t_rows, :] += jnp.where(own, nn(ds.astype(bf16), k), 0.0)
                s_t = nt(k, q)
                ds_t = nt(v, g) * s_t
                p_t = s_t * s_t + 0.5
                if masked:
                    ds_t = jnp.where(upper_triangle(block), ds_t, 0.0)
                    p_t = jnp.where(upper_triangle(block), p_t, 0.0)
                dk[s_rows, :] += nn(ds_t.astype(bf16), q)
                dv[s_rows, pl.ds(LANES * u, LANES)] += nn(p_t.astype(bf16), g[:, :LANES])

        def one(j):
            pair(j, j, True)
            sweep(j + 1, blocks, lambda i: pair(i, j, False))

        sweep(0, blocks, one)

        def finish(i):
            rows = rows_at(i, block)
            lane = lane_of((block, LANES))
            valid = (i * block + lax.broadcasted_iota(jnp.int32, (block, LANES), 0)) < valid_len
            keys = jnp.where(valid & (lane < HALF), dk[rows, :], 0.0)
            both = jnp.where(lane < HALF, dq[rows, :], pltpu.roll(keys, HALF, 1))
            out[rows, :LANES] = (both * (2.0 * alpha)).astype(bf16)
            for u in range(units):
                grad = dv[rows, pl.ds(LANES * u, LANES)]
                out[rows, pl.ds(LANES * (u + 1), LANES)] = jnp.where(valid, grad, 0.0).astype(bf16)

        sweep(0, blocks, finish)

    return pl.pallas_call(
        kernel,
        out_shape=jax.ShapeDtypeStruct((total, LANES * (units + 1)), bf16),
        in_specs=[pl.BlockSpec(memory_space=pltpu.SMEM)] * 2
        + [pl.BlockSpec(memory_space=pl.ANY)] * (2 * count)
        + [pl.BlockSpec(memory_space=pltpu.VMEM)] * 2,
        out_specs=pl.BlockSpec(memory_space=pltpu.VMEM),
        scratch_shapes=[
            pltpu.VMEM((total, LANES * (units + 1)), bf16),
            pltpu.VMEM((units, total, LANES), bf16),
            pltpu.VMEM((total, LANES), bf16),
            pltpu.VMEM((units, total, 2 * LANES), bf16),
            pltpu.VMEM((total, LANES * units), bf16),
            pltpu.VMEM((units, total, 2 * LANES), bf16),
            pltpu.VMEM((total, LANES), f32),
            pltpu.VMEM((total, LANES), f32),
            pltpu.VMEM((total, LANES * units), f32),
            pltpu.SemaphoreType.DMA((2 * count,)),
        ],
        compiler_params=pltpu.CompilerParams(vmem_limit_bytes=56 * 1024 * 1024),
        cost_estimate=pl.CostEstimate(
            flops=units * total * total * 1200, bytes_accessed=total * 8192, transcendentals=0
        ),
    )(jnp.stack(sources).astype(jnp.int32), length, *pieces, *d_pieces, attn, den)


def weight_grad(links, left, right):
    tokens, width = left.shape
    block = right.shape[1] // links.nz

    def kernel(place, left_ref, right_ref, out_ref):
        out_ref[0] = tn(left_ref[...], right_ref[...]).astype(bf16)

    return pl.pallas_call(
        kernel,
        out_shape=jax.ShapeDtypeStruct((links.nz, width, block), bf16),
        grid_spec=pltpu.PrefetchScalarGridSpec(
            num_scalar_prefetch=1,
            grid=(links.nz,),
            in_specs=[
                pl.BlockSpec((tokens, width), lambda j, at: (0, 0)),
                pl.BlockSpec((tokens, block), lambda j, at: (0, at[j])),
            ],
            out_specs=pl.BlockSpec((1, width, block), lambda j, at: (j, 0, 0)),
        ),
        compiler_params=pltpu.CompilerParams(vmem_limit_bytes=56 * 1024 * 1024),
        cost_estimate=pl.CostEstimate(
            flops=2 * tokens * width * right.shape[1],
            bytes_accessed=2 * (tokens * width + right.size + width * right.shape[1]),
            transcendentals=0,
        ),
    )(jnp.stack([links.behind(j) for j in range(links.nz)]).astype(jnp.int32), left, right)


def on_device(
    hidden_in,
    lengths,
    q_weight,
    k_weight,
    v_weight,
    out_weight,
    conv_weight,
    norm_attn,
    gate_weight,
    up_weight,
    down_weight,
    norm_mlp,
    cotangent,
):
    links = Links()
    nb, nz, ns = (links.nb, links.nz, links.ns)
    rows, local, width = hidden_in.shape
    tokens = rows * local
    own = width // (nb * ns)
    groups = ns // rows
    units = HEADS // groups
    value_dim = width // HEADS
    lag = KERNEL - 1
    hidden_dim = gate_weight.shape[1]
    slice_dim = hidden_dim // (2 * nb)
    seq_len = local * ns

    def by_plane(v):
        return v.reshape(v.shape[:-1] + (nb, nz, 2 * own)).swapaxes(-3, -2).reshape(v.shape)

    def by_owner(v):
        return v.reshape(v.shape[:-1] + (nz, nb, 2 * own)).swapaxes(-3, -2).reshape(v.shape)

    own_lengths = lax.dynamic_slice_in_dim(lengths, links.b * rows, rows, 0)
    total_valid = jnp.sum(lengths).astype(f32)

    small = jnp.concatenate([norm_attn[None], norm_mlp[None], conv_weight.T], axis=0)
    items, places = links.gather_all(small)
    small_all = jnp.zeros((nz * nb * 2,) + small.shape, bf16)
    for (value, k), at in zip(items, places):
        small_all = lax.dynamic_update_slice_in_dim(small_all, value[k][None], at, 0)
    small_all = small_all.swapaxes(0, 1).reshape(small.shape[0], width).astype(f32)
    gain_attn, gain_mlp, taps = (small_all[0], small_all[1], small_all[2:])

    def paired(q_part, k_part):
        pad = ((0, 0), (0, 0), (0, HALF - units * FEAT))
        q_part = jnp.pad(q_part.reshape(-1, groups, units * FEAT), pad)
        k_part = jnp.pad(k_part.reshape(-1, groups, units * FEAT), pad)
        return jnp.concatenate([q_part, k_part], axis=-1).reshape(-1, groups * LANES)

    packed = jnp.concatenate([paired(q_weight, k_weight), v_weight], axis=1)
    w_in = join_rows(*links.gather_all(packed), own, packed.shape[1])
    w_out = join_rows(*links.gather_all(out_weight.T), own, width)

    x = by_plane(hidden_in)
    edge = lax.ppermute(x[:, local - lag :], "seq", [(s, s + 1) for s in range(ns - 1)])
    inputs = x.astype(f32)
    extended = rms_norm(jnp.concatenate([edge.astype(f32), inputs], axis=1), gain_attn)
    mixed = sum(taps[j] * extended[:, lag - j : lag - j + local] for j in range(KERNEL))
    c_low = mixed.astype(bf16).reshape(tokens, width)
    proj = nn(c_low, w_in)
    qk_width = groups * LANES
    qk = (proj[:, :qk_width] * alpha).astype(bf16).reshape(rows, local, groups, LANES)
    v_low = proj[:, qk_width:].astype(bf16).reshape(rows, local, groups, units * value_dim)
    outgoing = jnp.concatenate([qk, v_low], axis=-1).swapaxes(1, 2)
    outgoing = outgoing.reshape((ns, local, LANES * (units + 1)))
    pieces, sources = links.exchange_seq(outgoing)
    row_length = pick(own_lengths, links.seq // groups)
    block = min(256, seq_len)
    y_units, attn_units, den_units = attend(pieces, sources, row_length[None], units, block)
    y_pieces, y_sources = links.exchange_seq(y_units.reshape(ns, local, units * value_dim))

    def merge_heads(parts, froms):
        whole = join_lead(parts, froms).reshape(rows, groups, local, -1)
        return whole.swapaxes(1, 2).reshape(tokens, -1)

    y_low = merge_heads(y_pieces, y_sources)
    counted = (jnp.arange(seq_len, dtype=jnp.int32) < row_length)[:, None]
    den_sum = jnp.sum(jnp.where(counted, den_units[:, :units], 0.0))
    den_mean = links.sum_all(den_sum[None])[0] / (HEADS * seq_len * total_valid)

    def share_out(stacked):
        count = stacked.shape[0]
        by_slice = stacked.reshape(count, nb, 2, slice_dim, own)
        keep, got = (pick(by_slice, links.c, 2), links.core(pick(by_slice, links.c ^ 1, 2)))
        both = jnp.where(
            links.c == 0,
            jnp.concatenate([keep, got], axis=-1),
            jnp.concatenate([got, keep], axis=-1),
        )
        parts = [pick(both, links.b ^ d, 1) for d in range(nb)]
        parts = [links.across(p, d) if d else p for d, p in enumerate(parts)]
        plane = join_lanes(parts, [links.b ^ d for d in range(nb)])
        chain = [plane]
        for _ in range(nz - 1):
            chain.append(links.ring(chain[-1]))
        return join_lanes(chain, [links.behind(k) for k in range(nz)])

    gate_up = share_out(jnp.stack([gate_weight.T, up_weight.T]))
    down_cols = share_out(down_weight[None])[0]
    gate_cols, up_cols = (gate_up[0], gate_up[1])

    cot = by_plane(cotangent).reshape(tokens, width)
    cot_all = links.gather_plane(cot)

    resid_mid = inputs.reshape(tokens, width) + nt(y_low, w_out)
    n2_low = rms_norm(resid_mid, gain_mlp).astype(bf16)
    n2_all = links.gather_plane(n2_low)
    gate_act, up_act = (nt(n2_all, gate_cols), nt(n2_all, up_cols))
    sigma = jax.nn.sigmoid(gate_act)
    hidden_act = (gate_act * sigma * up_act).astype(bf16)
    d_hid = nt(cot_all, down_cols)
    d_gate = (d_hid * up_act * sigma * (1.0 + gate_act * (1.0 - sigma))).astype(bf16)
    d_up = (d_hid * gate_act * sigma).astype(bf16)
    back = (nn(d_gate, gate_cols) + nn(d_up, up_cols)).astype(bf16)
    d_n2 = links.scatter_plane(back.reshape(2, nb, tokens, width))
    down_part = nn(hidden_act, down_cols).astype(bf16)
    down_sum = links.scatter_plane(down_part.reshape(2, nb, tokens, width))
    hidden_out = by_owner((resid_mid + down_sum).astype(bf16)).reshape(rows, local, width)

    def give_back(*pairs):
        grads = [weight_grad(links, left, right) for left, right in pairs]
        sums = [
            links.scatter_ring([g[j] for j in range(nz)]).astype(bf16) for g in grads
        ]
        stacked = jnp.stack(sums).reshape(len(pairs), slice_dim, nb, 2 * own)
        stacked = jnp.moveaxis(stacked, 2, 0)
        parts = [pick(stacked, links.b ^ d) for d in range(nb)]
        parts = [links.across(p, d) if d else p for d, p in enumerate(parts)]
        mine = join_lead(parts, [links.b ^ d for d in range(nb)])
        mine = mine.reshape(nb, len(pairs), slice_dim, 2, own)
        keep, got = (pick(mine, links.c, 3), links.core(pick(mine, links.c ^ 1, 3)))
        both = jnp.where(links.c == 0, jnp.stack([keep, got], 1), jnp.stack([got, keep], 1))
        both = jnp.moveaxis(both, 2, 0).reshape(len(pairs), hidden_dim, own)
        return [both[i].astype(f32) for i in range(len(pairs))]

    (grad_down,) = give_back((hidden_act, cot_all))
    grad_gate, grad_up = (g.T for g in give_back((d_gate, n2_all), (d_up, n2_all)))

    _, norm_pull = jax.vjp(rms_norm, resid_mid, gain_mlp)
    d_mid_norm, grad_gain_mlp = norm_pull(d_n2)
    d_mid = cot.astype(f32) + d_mid_norm
    d_attn = d_mid.astype(bf16)
    d_y = nn(d_attn, w_out).astype(bf16).reshape(rows, local, groups, units * value_dim)
    d_pieces, _ = links.exchange_seq(d_y.swapaxes(1, 2).reshape(ns, local, units * value_dim))
    d_units = attend_back(
        pieces, sources, row_length[None], d_pieces, attn_units, den_units, units, block
    )
    back_pieces, back_sources = links.exchange_seq(d_units.reshape(ns, local, LANES * (units + 1)))
    d_all = join_lead(back_pieces, back_sources).reshape(rows, groups, local, -1).swapaxes(1, 2)
    d_proj = jnp.concatenate(
        [
            d_all[..., :LANES].reshape(tokens, qk_width),
            d_all[..., LANES:].reshape(tokens, width),
        ],
        axis=1,
    )

    def by_device(v):
        return v.reshape((nz, nb, 2, own) + v.shape[1:])

    grad_out = links.scatter_all(by_device(tn(d_attn, y_low).astype(bf16))).T
    packed_grad = links.scatter_all(by_device(tn(c_low, d_proj).astype(bf16)))
    grad_v = packed_grad[:, qk_width:]
    grad_qk = packed_grad[:, :qk_width].reshape(own, groups, 2, HALF)[..., : units * FEAT]
    grad_q = grad_qk[:, :, 0].reshape(own, HEADS * FEAT)
    grad_k = grad_qk[:, :, 1].reshape(own, HEADS * FEAT)

    d_c = nt(d_proj, w_in).reshape(rows, local, width)
    next_edge = lax.ppermute(
        d_c[:, :lag].astype(bf16), "seq", [(s + 1, s) for s in range(ns - 1)]
    ).astype(f32)
    d_extended = jnp.concatenate([d_c, next_edge], axis=1)
    d_n1 = sum(taps[j] * d_extended[:, j : j + local] for j in range(KERNEL))
    conv_rows = [
        jnp.sum(d_c * extended[:, lag - j : lag - j + local], axis=(0, 1)) for j in range(KERNEL)
    ]
    _, first_pull = jax.vjp(rms_norm, inputs, gain_attn)
    d_inputs, grad_gain_attn = first_pull(d_n1)
    hidden_grad = by_owner(d_mid.reshape(rows, local, width) + d_inputs)
    small_grads = jnp.stack([grad_gain_attn, grad_gain_mlp] + conv_rows)
    small_grads = jnp.moveaxis(small_grads.reshape(2 + KERNEL, nz, nb, 2, own), 0, 3)
    small_sum = links.scatter_all(small_grads)
    return (
        hidden_out,
        hidden_grad,
        grad_q,
        grad_k,
        grad_v,
        grad_out,
        small_sum[2:].T,
        small_sum[0],
        grad_gate,
        grad_up,
        grad_down,
        small_sum[1],
        den_mean,
    )


def solution(mesh):
    both = ("batch", "seq")
    tokens = P("batch", "seq", None)
    by_row, by_col, vector = (P(both, None), P(None, both), P(both))
    return jax.shard_map(
        on_device,
        mesh=mesh,
        in_specs=(
            tokens,
            P(),
            by_row,
            by_row,
            by_row,
            by_col,
            by_row,
            vector,
            by_row,
            by_row,
            by_col,
            vector,
            tokens,
        ),
        out_specs=(
            tokens,
            tokens,
            by_row,
            by_row,
            by_row,
            by_col,
            by_row,
            vector,
            by_row,
            by_row,
            by_col,
            vector,
            P(),
        ),
        check_vma=False,
    )
```
